512 devices in a mesh: gx: 32 (over z_lo, y), gy: 16 (over z_hi, x, core).
Axes of the slice: x: 4, y: 8, z: 8 (z_hi: 2, z_lo: 4; z = z_hi * 4 + z_lo), core: 2. Of those that a mesh axis runs over, the one named last changes fastest.
Arguments:
- images: bfloat16 [262144, 1152], P(('gx', 'gy')), may hold values from -6 to 6
- texts: bfloat16 [262144, 1152], P(('gx', 'gy')), may hold values from -6 to 6
- log_scale: float32 [1], replicated, may hold values from 1.5 to 2.5
- bias: float32 [1], replicated, may hold values from -1 to 1
Outputs:
- image_grad: bfloat16 [262144, 1152], P(('gx', 'gy'))
- text_grad: bfloat16 [262144, 1152], P(('gx', 'gy'))
The draws below stay inside these ranges and needn't reach their ends.
All inputs are finite; a program needn't handle non-finite values.
Results may differ from the reference program's by a relative error of at most 0.015.
Values may be sent and summed in bfloat16 or wider, within the bound.
A program may use at most 64 MiB of HBM per device.

```python
import jax
import jax.numpy as jnp
from jax import lax

D = 1152
TOK_DEV = 512
STEPS = 2
TOKENS = 262144


def block_scale(rng, extent, shards, smallest, top_value):
    loudness = 1.0
    for position, shards_of in shards:
        heights = jax.random.uniform(jax.random.fold_in(jax.random.fold_in(rng, 6), position), (shards_of,), jnp.float32, smallest / len(shards), top_value / len(shards))
        loudness = loudness * jnp.repeat(jnp.exp(heights), extent[position] // shards_of).reshape((-1,) + (1,) * (len(extent) - 1 - position))
    return loudness


def centred(own_key, shape, scale, bound, cuts=(), kind=jnp.bfloat16):
    loudness = block_scale(own_key, shape, cuts, -0.22, 0.18) if cuts else 1.0
    drawn = jax.random.normal(own_key, shape, jnp.float32) * scale * loudness
    return jnp.minimum(jnp.maximum(drawn, -bound), bound).astype(kind)


def setup_inputs(seed: int = 0) -> dict:
    key_list = jax.random.split(jax.random.key(seed), 5)
    images = centred(key_list[0], (TOKENS, D), 1.0, 6.0, ((0, 512),))
    texts = centred(key_list[1], (TOKENS, D), 1.0, 6.0, ((0, 512),))
    log_scale = jnp.clip(jax.random.uniform(key_list[2], (1,), jnp.float32, 1.5, 2.5), 1.5, 2.5)
    bias = jnp.clip(jax.random.uniform(key_list[3], (1,), jnp.float32, -1.0, 1.0), -1.0, 1.0)
    return dict(images=images, texts=texts, log_scale=log_scale, bias=bias)


def normalize(raw):
    values = raw.astype(jnp.float32)
    inverse = lax.rsqrt(lax.optimization_barrier(jnp.sum(values * values, axis=-1, keepdims=True)) + 1e-06)
    return (values * inverse, inverse)

def coefficient(image_block, text_block, shift_count, scale, offset):
    logits = scale * lax.dot_general(image_block, text_block, (((1,), (1,)), ((), ())), preferred_element_type=jnp.float32) + offset
    rows = image_block.shape[0]
    if shift_count == 0:
        same = lax.broadcasted_iota(jnp.int32, (rows, rows), 0) == lax.broadcasted_iota(jnp.int32, (rows, rows), 1)
        label = jnp.where(same, 1.0, -1.0).astype(jnp.float32)
    else:
        label = -jnp.ones((rows, rows), jnp.float32)
    grad = -label * jax.nn.sigmoid(-label * logits)
    return (scale * grad / (STEPS + 1)).astype(jnp.bfloat16)

def back_norm(unit, inverse, grad):
    return ((grad - unit * lax.optimization_barrier(jnp.sum(unit * grad, axis=-1, keepdims=True))) * inverse).astype(jnp.bfloat16)

def reference(images, texts, log_scale, bias):
    image_unit, image_inv = normalize(images)
    text_unit, text_inv = normalize(texts)
    image_low = image_unit.astype(jnp.bfloat16)
    text_low = text_unit.astype(jnp.bfloat16)
    count = TOKENS // TOK_DEV
    image_blocks = image_low.reshape(count, TOK_DEV, D)
    text_blocks = text_low.reshape(count, TOK_DEV, D)
    scale = jnp.exp(log_scale[0])
    offset = bias[0]

    def one_block(index):
        image_grad = jnp.zeros((TOK_DEV, D), jnp.float32)
        text_grad = jnp.zeros((TOK_DEV, D), jnp.float32)
        own_image = image_blocks[index]
        own_text = text_blocks[index]
        for shift_count in range(STEPS + 1):
            earlier = text_blocks[(index - shift_count) % count]
            coef = coefficient(own_image, earlier, shift_count, scale, offset)
            image_grad = image_grad + jnp.dot(coef, earlier, preferred_element_type=jnp.float32)
            later = image_blocks[(index + shift_count) % count]
            coef_later = coefficient(later, own_text, shift_count, scale, offset)
            text_grad = text_grad + lax.dot_general(coef_later, later, (((0,), (0,)), ((), ())), preferred_element_type=jnp.float32)
        return (image_grad, text_grad)
    image_parts, text_parts = lax.map(one_block, jnp.arange(count, dtype=jnp.int32))
    unit_image_grad = image_parts.reshape(TOKENS, D)
    unit_text_grad = text_parts.reshape(TOKENS, D)
    return (back_norm(image_unit, image_inv, unit_image_grad), back_norm(text_unit, text_inv, unit_text_grad))
```

```python
import functools

import jax
import jax.numpy as jnp
from jax import lax
from jax.experimental import pallas as pl
from jax.experimental.pallas import tpu as pltpu
from jax.sharding import PartitionSpec as P

STEPS = 2
MESH = pl.DeviceIdType.MESH
CHUNK = 128
RELAYED = 0


def kernel(
    n, scale_ref, bias_ref, images_ref, texts_ref, image_out, text_out,
    raw, low, inverse, total, far, near, relay, result,
    load_sem, store_sem, far_send, far_recv, near_send, near_recv, pass_send, pass_recv,
):
    rows, width = raw.shape[1:]
    chunks = rows // CHUNK
    gx, gy = lax.axis_index("gx"), lax.axis_index("gy")
    inner = lax.axis_size("gy")
    me = gx * inner + gy
    core = lax.rem(gy, 2)
    x = lax.rem(gy // 2, 4)

    def at(distance):
        there = lax.rem(me + distance + n, n)
        return (there // inner, lax.rem(there, inner))

    sibling = (gx, gy + 1 - 2 * core)
    after, before = at(2), at(-2)

    barrier = pltpu.get_barrier_semaphore()
    for partner in (after, before, sibling):
        pl.semaphore_signal(barrier, inc=1, device_id=partner, device_id_type=MESH)

    loads = [
        pltpu.make_async_copy(ref, raw.at[side], load_sem.at[side])
        for side, ref in enumerate((images_ref, texts_ref))
    ]
    for load in loads:
        load.start()
    for side in range(2):
        loads[side].wait()

        @pl.loop(0, chunks)
        def _(j):
            span = pl.ds(j * CHUNK, CHUNK)
            values = raw[side, span, :].astype(jnp.float32)
            inv = lax.rsqrt(jnp.sum(values * values, axis=-1, keepdims=True) + 1e-06)
            inverse[side, span, :] = inv
            low[side, span, :] = (values * inv).astype(jnp.bfloat16)

    pl.semaphore_wait(barrier, 3)

    def far_copy(side, j, partner):
        span = pl.ds(j * CHUNK, CHUNK)
        return pltpu.make_async_remote_copy(
            src_ref=low.at[1 - side, span],
            dst_ref=far.at[side, span],
            send_sem=far_send.at[side, j],
            recv_sem=far_recv.at[side, j],
            device_id=partner,
            device_id_type=MESH,
        )

    def near_copy(source, side, j):
        span = pl.ds(j * CHUNK, CHUNK)
        return pltpu.make_async_remote_copy(
            src_ref=source.at[span],
            dst_ref=near.at[side, span],
            send_sem=near_send.at[side, j],
            recv_sem=near_recv.at[side, j],
            device_id=sibling,
            device_id_type=MESH,
        )

    @pl.loop(0, chunks)
    def _(j):
        far_copy(0, j, after).start()
        far_copy(1, j, before).start()

    @pl.loop(0, chunks)
    def _(j):
        near_copy(low.at[1 - core], core, j).start()

    scale = jnp.exp(jnp.full((1, CHUNK), scale_ref[0], jnp.float32))
    offset = bias_ref[0]
    third = scale / (STEPS + 1)

    def weigh(side, other, j, own):
        logits = scale * lax.dot_general(
            low[side], other, (((1,), (1,)), ((), ())), preferred_element_type=jnp.float32
        ) + offset
        if own:
            same = lax.broadcasted_iota(jnp.int32, logits.shape, 0) == j * CHUNK + (
                lax.broadcasted_iota(jnp.int32, logits.shape, 1)
            )
            part = jax.nn.sigmoid(jnp.where(same, -logits, logits))
            coef = (jnp.where(same, -part, part) * third).astype(jnp.bfloat16)
        else:
            coef = (jax.nn.sigmoid(logits) * third).astype(jnp.bfloat16)
        return jnp.dot(coef, other, preferred_element_type=jnp.float32)

    for side in range(2):

        @pl.loop(0, chunks)
        def _(j):
            part = weigh(side, low[1 - side, pl.ds(j * CHUNK, CHUNK), :], j, True)

            @pl.when(j == 0)
            def _():
                total[side] = part

            @pl.when(j > 0)
            def _():
                total[side] += part

    def add_near(side, j):
        near_copy(low.at[0], side, j).wait_recv()
        total[side] += weigh(side, near[side, pl.ds(j * CHUNK, CHUNK), :], j, False)

    @pl.loop(0, chunks)
    def _(j):
        add_near(1 - core, j)

    @pl.loop(0, chunks)
    def _(j):
        for side in range(2):
            far_copy(side, j, after).wait_recv()

            @pl.when(core == 1 - side)
            def _():
                near_copy(far.at[side], side, j).start()

            total[side] += weigh(side, far[side, pl.ds(j * CHUNK, CHUNK), :], j, False)
        add_near(core, j)

    for side, out in enumerate((image_out, text_out)):

        @pl.loop(0, chunks)
        def _(j):
            span = pl.ds(j * CHUNK, CHUNK)
            inv = inverse[side, span, :]
            unit = raw[side, span, :].astype(jnp.float32) * inv
            grad = total[side, span, :]
            along = jnp.sum(unit * grad, axis=-1, keepdims=True)
            result[side, span, :] = ((grad - unit * along) * inv).astype(jnp.bfloat16)

        pltpu.make_async_copy(result.at[side], out, store_sem.at[side]).start()

    @pl.loop(0, chunks)
    def _(j):
        for side in range(2):
            far_copy(side, j, after).wait_send()
            near_copy(low.at[0], side, j).wait_send()

    for side, out in enumerate((image_out, text_out)):
        pltpu.make_async_copy(result.at[side], out, store_sem.at[side]).wait()


def on_device(images, texts, log_scale, bias):
    rows, width = images.shape
    chunks = rows // CHUNK
    n = lax.axis_size("gx") * lax.axis_size("gy")
    block = (2, rows, width)
    dma = pltpu.SemaphoreType.DMA
    return pl.pallas_call(
        functools.partial(kernel, n),
        out_shape=[jax.ShapeDtypeStruct((rows, width), jnp.bfloat16)] * 2,
        in_specs=[pl.BlockSpec(memory_space=pltpu.SMEM)] * 2 + [pl.BlockSpec(memory_space=pl.ANY)] * 2,
        out_specs=[pl.BlockSpec(memory_space=pl.ANY)] * 2,
        scratch_shapes=[
            pltpu.VMEM(block, jnp.bfloat16),
            pltpu.VMEM(block, jnp.bfloat16),
            pltpu.VMEM((2, rows, 1), jnp.float32),
            pltpu.VMEM(block, jnp.float32),
            pltpu.VMEM(block, jnp.bfloat16),
            pltpu.VMEM(block, jnp.bfloat16),
            pltpu.VMEM((rows, width), jnp.bfloat16),
            pltpu.VMEM(block, jnp.bfloat16),
            dma((2,)),
            dma((2,)),
            dma((2, chunks)),
            dma((2, chunks)),
            dma((2, chunks)),
            dma((2, chunks)),
            dma((chunks,)),
            dma((chunks,)),
        ],
        compiler_params=pltpu.CompilerParams(
            collective_id=0, has_side_effects=True, vmem_limit_bytes=48 * 1024 * 1024
        ),
        cost_estimate=pl.CostEstimate(
            flops=24 * rows * rows * width, bytes_accessed=8 * rows * width, transcendentals=6 * rows * rows
        ),
        name="contrast",
    )(log_scale, bias, images, texts)


def solution(mesh):
    return jax.shard_map(
        on_device,
        mesh=mesh,
        in_specs=(P(("gx", "gy"), None), P(("gx", "gy"), None), P(), P()),
        out_specs=(P(("gx", "gy"), None), P(("gx", "gy"), None)),
        check_vma=False,
    )
```

```python
import functools

import jax
import jax.numpy as jnp
from jax import lax
from jax.experimental import pallas as pl
from jax.experimental.pallas import tpu as pltpu
from jax.sharding import PartitionSpec as P

STEPS = 2
MESH = pl.DeviceIdType.MESH
CHUNK = 256
PIECES = 8
GROUP = 4
RELAYED = 2


def kernel(
    n, scale_ref, bias_ref, images_ref, texts_ref, image_out, text_out,
    raw, low, inverse, total, far, near, relay, result,
    load_sem, store_sem, far_send, far_recv, near_send, near_recv, pass_send, pass_recv,
):
    rows, width = raw.shape[1:]
    chunks = rows // CHUNK
    gx, gy = lax.axis_index("gx"), lax.axis_index("gy")
    inner = lax.axis_size("gy")
    me = gx * inner + gy
    core = lax.rem(gy, 2)
    x = lax.rem(gy // 2, 4)

    def at(distance):
        there = lax.rem(me + distance + n, n)
        return (there // inner, lax.rem(there, inner))

    sibling = (gx, gy + 1 - 2 * core)
    after, before = at(2), at(-2)

    barrier = pltpu.get_barrier_semaphore()
    for partner in (after, before, sibling):
        pl.semaphore_signal(barrier, inc=1, device_id=partner, device_id_type=MESH)

    loads = [
        pltpu.make_async_copy(ref, raw.at[side], load_sem.at[side])
        for side, ref in enumerate((images_ref, texts_ref))
    ]
    for load in loads:
        load.start()
    for side in range(2):
        loads[side].wait()

        @pl.loop(0, chunks)
        def _(j):
            span = pl.ds(j * CHUNK, CHUNK)
            values = raw[side, span, :].astype(jnp.float32)
            inv = lax.rsqrt(jnp.sum(values * values, axis=-1, keepdims=True) + 1e-06)
            inverse[side, span, :] = inv
            low[side, span, :] = (values * inv).astype(jnp.bfloat16)

    pl.semaphore_wait(barrier, 3)

    size = rows // PIECES
    edge = jnp.logical_or(x == 0, x == 3)
    middle = jnp.logical_not(edge)
    passing = jnp.where(x >= 2, 0, 1)
    inward = at(jnp.where(x == 3, -2, 2))
    onward = at(jnp.where(x == 2, 4, -4))

    def far_copy(side, j, partner):
        span = pl.ds(j * size, size)
        return pltpu.make_async_remote_copy(
            src_ref=low.at[1 - side, span],
            dst_ref=far.at[side, span],
            send_sem=far_send.at[side, j],
            recv_sem=far_recv.at[side, j],
            device_id=partner,
            device_id_type=MESH,
        )

    def relay_copy(j):
        span = pl.ds(j * size, size)
        return pltpu.make_async_remote_copy(
            src_ref=low.at[1 - passing, span],
            dst_ref=relay.at[span],
            send_sem=far_send.at[passing, j],
            recv_sem=pass_recv.at[j],
            device_id=inward,
            device_id_type=MESH,
        )

    def onward_copy(j):
        span = pl.ds(j * size, size)
        return pltpu.make_async_remote_copy(
            src_ref=relay.at[span],
            dst_ref=far.at[passing, span],
            send_sem=pass_send.at[j],
            recv_sem=far_recv.at[passing, j],
            device_id=onward,
            device_id_type=MESH,
        )

    def near_copy(source, side, j):
        span = pl.ds(j * size, size)
        return pltpu.make_async_remote_copy(
            src_ref=source.at[span],
            dst_ref=near.at[side, span],
            send_sem=near_send.at[side, j],
            recv_sem=near_recv.at[side, j],
            device_id=sibling,
            device_id_type=MESH,
        )

    def relayed(j):
        return lax.rem(j, GROUP) < RELAYED

    @pl.loop(0, PIECES)
    def _(j):
        @pl.when(jnp.logical_and(edge, relayed(j)))
        def _():
            relay_copy(j).start()

    @pl.loop(0, PIECES)
    def _(j):
        for side, partner in enumerate((after, before)):
            through = jnp.logical_and(x == 3 - 3 * side, relayed(j))

            @pl.when(jnp.logical_not(through))
            def _():
                far_copy(side, j, partner).start()

    @pl.loop(0, PIECES)
    def _(j):
        near_copy(low.at[1 - core], core, j).start()

    @pl.loop(0, PIECES)
    def _(j):
        @pl.when(jnp.logical_and(middle, relayed(j)))
        def _():
            relay_copy(j).wait_recv()
            onward_copy(j).start()

    scale = jnp.exp(jnp.full((1, CHUNK), scale_ref[0], jnp.float32))
    offset = bias_ref[0]
    third = scale / (STEPS + 1)

    def weigh(side, other, j, own):
        logits = scale * lax.dot_general(
            low[side], other, (((1,), (1,)), ((), ())), preferred_element_type=jnp.float32
        ) + offset
        if own:
            same = lax.broadcasted_iota(jnp.int32, logits.shape, 0) == j * CHUNK + (
                lax.broadcasted_iota(jnp.int32, logits.shape, 1)
            )
            part = jax.nn.sigmoid(jnp.where(same, -logits, logits))
            coef = (jnp.where(same, -part, part) * third).astype(jnp.bfloat16)
        else:
            coef = (jax.nn.sigmoid(logits) * third).astype(jnp.bfloat16)
        return jnp.dot(coef, other, preferred_element_type=jnp.float32)

    for side in range(2):

        @pl.loop(0, chunks)
        def _(j):
            part = weigh(side, low[1 - side, pl.ds(j * CHUNK, CHUNK), :], j, True)

            @pl.when(j == 0)
            def _():
                total[side] = part

            @pl.when(j > 0)
            def _():
                total[side] += part

    def add_near(side, j):
        for i in range(GROUP):
            near_copy(low.at[0], side, j * GROUP + i).wait_recv()
        total[side] += weigh(side, near[side, pl.ds(j * CHUNK, CHUNK), :], j, False)

    @pl.loop(0, chunks)
    def _(j):
        add_near(1 - core, j)

    @pl.loop(0, chunks)
    def _(j):
        for side in range(2):
            for i in range(GROUP):
                far_copy(side, j * GROUP + i, after).wait_recv()

                @pl.when(core == 1 - side)
                def _():
                    near_copy(far.at[side], side, j * GROUP + i).start()

            total[side] += weigh(side, far[side, pl.ds(j * CHUNK, CHUNK), :], j, False)
        add_near(core, j)

    for side, out in enumerate((image_out, text_out)):

        @pl.loop(0, chunks)
        def _(j):
            span = pl.ds(j * CHUNK, CHUNK)
            inv = inverse[side, span, :]
            unit = raw[side, span, :].astype(jnp.float32) * inv
            grad = total[side, span, :]
            along = jnp.sum(unit * grad, axis=-1, keepdims=True)
            result[side, span, :] = ((grad - unit * along) * inv).astype(jnp.bfloat16)

        pltpu.make_async_copy(result.at[side], out, store_sem.at[side]).start()

    @pl.loop(0, PIECES)
    def _(j):
        for side in range(2):
            far_copy(side, j, after).wait_send()
            near_copy(low.at[0], side, j).wait_send()

        @pl.when(jnp.logical_and(middle, relayed(j)))
        def _():
            onward_copy(j).wait_send()

    for side, out in enumerate((image_out, text_out)):
        pltpu.make_async_copy(result.at[side], out, store_sem.at[side]).wait()


def on_device(images, texts, log_scale, bias):
    rows, width = images.shape
    n = lax.axis_size("gx") * lax.axis_size("gy")
    block = (2, rows, width)
    dma = pltpu.SemaphoreType.DMA
    return pl.pallas_call(
        functools.partial(kernel, n),
        out_shape=[jax.ShapeDtypeStruct((rows, width), jnp.bfloat16)] * 2,
        in_specs=[pl.BlockSpec(memory_space=pltpu.SMEM)] * 2 + [pl.BlockSpec(memory_space=pl.ANY)] * 2,
        out_specs=[pl.BlockSpec(memory_space=pl.ANY)] * 2,
        scratch_shapes=[
            pltpu.VMEM(block, jnp.bfloat16),
            pltpu.VMEM(block, jnp.bfloat16),
            pltpu.VMEM((2, rows, 1), jnp.float32),
            pltpu.VMEM(block, jnp.float32),
            pltpu.VMEM(block, jnp.bfloat16),
            pltpu.VMEM(block, jnp.bfloat16),
            pltpu.VMEM((rows, width), jnp.bfloat16),
            pltpu.VMEM(block, jnp.bfloat16),
            dma((2,)),
            dma((2,)),
            dma((2, PIECES)),
            dma((2, PIECES)),
            dma((2, PIECES)),
            dma((2, PIECES)),
            dma((PIECES,)),
            dma((PIECES,)),
        ],
        compiler_params=pltpu.CompilerParams(
            collective_id=0, has_side_effects=True, vmem_limit_bytes=48 * 1024 * 1024
        ),
        cost_estimate=pl.CostEstimate(
            flops=24 * rows * rows * width, bytes_accessed=8 * rows * width, transcendentals=6 * rows * rows
        ),
        name="contrast",
    )(log_scale, bias, images, texts)


def solution(mesh):
    return jax.shard_map(
        on_device,
        mesh=mesh,
        in_specs=(P(("gx", "gy"), None), P(("gx", "gy"), None), P(), P()),
        out_specs=(P(("gx", "gy"), None), P(("gx", "gy"), None)),
        check_vma=False,
    )
```

```python
import functools

import jax
import jax.numpy as jnp
from jax import lax
from jax.experimental import pallas as pl
from jax.experimental.pallas import tpu as pltpu
from jax.sharding import PartitionSpec as P

STEPS = 2
MESH = pl.DeviceIdType.MESH
PIECES = 8
GROUP = 4
RELAYED = 2
AHEAD = 4


def kernel(
    n, scale_ref, bias_ref, images_ref, texts_ref, image_out, text_out,
    raw, low, inverse, total, far, near, relay, bend,
    load_sem, far_send, far_recv, near_send, near_recv, pass_send, pass_recv,
    bend_send, bend_recv, go_sem,
):
    rows, width = raw.shape[1:]
    size = rows // PIECES
    chunk = size * GROUP
    gx, gy = lax.axis_index("gx"), lax.axis_index("gy")
    inner = lax.axis_size("gy")
    me = gx * inner + gy
    core = lax.rem(gy, 2)
    x = lax.rem(gy // 2, 4)
    edge = jnp.logical_or(x == 0, x == 3)
    middle = jnp.logical_not(edge)
    early = gy < inner // 2
    waits = jnp.logical_and(edge, early)
    opens = jnp.logical_and(edge, jnp.logical_not(early))

    def at(distance):
        there = lax.rem(me + distance + n, n)
        return (there // inner, lax.rem(there, inner))

    sibling = (gx, gy + 1 - 2 * core)
    after, before = at(2), at(-2)
    across = at(jnp.where(x == 3, 2, -2))
    helper = at(jnp.where(x == 3, -4, 4))
    helped = at(jnp.where(x == 1, 4, -4))
    onward = at(jnp.where(x == 1, 6, -6))
    passing = 1 - lax.rem(x, 2)

    y, z = lax.rem(gx, 8), gx // 8 + 4 * (gy // 8)
    forth, back = passing == 0, passing == 1
    bent = jnp.logical_or(
        jnp.logical_and(forth, jnp.logical_and(y == 7, z == 5)),
        jnp.logical_and(back, jnp.logical_and(y == 0, z == 2)),
    )
    bends = jnp.logical_and(z == 0, y == 7 * passing)
    corner = (7 * passing, lax.rem(gy, 8))
    bent_from = (jnp.where(forth, 15, 16), jnp.where(forth, lax.rem(gy, 8) + 8, lax.rem(gy, 8)))
    bent_to = (jnp.where(forth, 16, 15), jnp.where(forth, core, 14 + core))

    barrier = pltpu.get_barrier_semaphore()
    pl.semaphore_signal(barrier, inc=1, device_id=sibling, device_id_type=MESH)
    for partner, last in ((after, 3), (before, 0)):

        @pl.when(jnp.logical_not(jnp.logical_and(opens, x == last)))
        def _():
            pl.semaphore_signal(barrier, inc=1, device_id=partner, device_id_type=MESH)

    @pl.when(middle)
    def _():
        pl.semaphore_signal(barrier, inc=1, device_id=helped, device_id_type=MESH)

    @pl.when(bends)
    def _():
        pl.semaphore_signal(barrier, inc=1, device_id=bent_from, device_id_type=MESH)

    greetings = 3 + edge.astype(jnp.int32) - waits.astype(jnp.int32) + bent.astype(jnp.int32)

    def load(ref, index, g):
        span = pl.ds(g * chunk, chunk)
        return pltpu.make_async_copy(ref.at[span], raw.at[index, span], load_sem.at[index, g])

    first = jnp.where(opens, 1 - passing, passing)
    for turn in range(2):
        for index, ref in enumerate((images_ref, texts_ref)):

            @pl.when(index == (first if turn == 0 else 1 - first))
            def _():
                for g in range(rows // chunk):
                    load(ref, index, g).start()

    def wait_load(index, j):
        @pl.when(lax.rem(j, GROUP) == 0)
        def _():
            load(images_ref, index, j // GROUP).wait()

    def far_copy(side, j, partner):
        span = pl.ds(j * size, size)
        return pltpu.make_async_remote_copy(
            src_ref=low.at[1 - side, span],
            dst_ref=far.at[side, span],
            send_sem=far_send.at[side, j],
            recv_sem=far_recv.at[side, j],
            device_id=partner,
            device_id_type=MESH,
        )

    def relay_copy(j):
        span = pl.ds(j * size, size)
        return pltpu.make_async_remote_copy(
            src_ref=low.at[1 - passing, span],
            dst_ref=relay.at[span],
            send_sem=far_send.at[passing, j],
            recv_sem=pass_recv.at[j],
            device_id=helper,
            device_id_type=MESH,
        )

    def onward_copy(j):
        span = pl.ds(j * size, size)
        return pltpu.make_async_remote_copy(
            src_ref=relay.at[span],
            dst_ref=far.at[passing, span],
            send_sem=pass_send.at[j],
            recv_sem=far_recv.at[passing, j],
            device_id=onward,
            device_id_type=MESH,
        )

    def bent_copy(source, send_sem, j):
        span = pl.ds(j * size, size)
        return pltpu.make_async_remote_copy(
            src_ref=source.at[span],
            dst_ref=bend.at[span],
            send_sem=send_sem,
            recv_sem=bend_recv.at[j],
            device_id=corner,
            device_id_type=MESH,
        )

    def last_copy(j):
        span = pl.ds(j * size, size)
        return pltpu.make_async_remote_copy(
            src_ref=bend.at[span],
            dst_ref=far.at[passing, span],
            send_sem=bend_send.at[j],
            recv_sem=far_recv.at[passing, j],
            device_id=bent_to,
            device_id_type=MESH,
        )

    def near_copy(source, side, j):
        span = pl.ds(j * size, size)
        return pltpu.make_async_remote_copy(
            src_ref=source.at[span],
            dst_ref=near.at[side, span],
            send_sem=near_send.at[side, j],
            recv_sem=near_recv.at[side, j],
            device_id=sibling,
            device_id_type=MESH,
        )

    def relayed(j):
        return lax.rem(j, GROUP) < RELAYED

    def send_across(j):
        @pl.when(relayed(j))
        def _():
            relay_copy(j).start()

        straight = jnp.logical_not(relayed(j))

        @pl.when(jnp.logical_and(straight, jnp.logical_not(bent)))
        def _():
            far_copy(passing, j, across).start()

        @pl.when(jnp.logical_and(straight, bent))
        def _():
            bent_copy(low.at[1 - passing], far_send.at[passing, j], j).start()

    def bent_here(j):
        return jnp.logical_and(bends, relayed(j) == middle)

    def normalize(index, j):
        span = pl.ds(j * size, size)
        values = raw[index, span, :].astype(jnp.float32)
        inv = lax.rsqrt(jnp.sum(values * values, axis=-1, keepdims=True) + 1e-06)
        inverse[index, span, :] = inv
        low[index, span, :] = (values * inv).astype(jnp.bfloat16)

    def send_along(side, j):
        for fixed, partner in enumerate((after, before)):

            @pl.when(side == fixed)
            def _():
                far_copy(fixed, j, partner).start()

    def enter(j):
        @pl.when(j == 0)
        def _():
            pl.semaphore_wait(barrier, greetings)

            @pl.when(opens)
            def _():
                pl.semaphore_signal(go_sem, inc=1, device_id=across, device_id_type=MESH)

    @pl.loop(0, PIECES)
    def _(j):
        wait_load(first, j)
        normalize(first, j)
        enter(j)

        @pl.when(opens)
        def _():
            send_across(j)

        @pl.when(jnp.logical_or(middle, jnp.logical_and(waits, j < AHEAD)))
        def _():
            send_along(1 - first, j)

    @pl.loop(0, PIECES)
    def _(j):
        wait_load(1 - first, j)
        normalize(1 - first, j)

        @pl.when(jnp.logical_or(middle, opens))
        def _():
            send_along(first, j)

        near_copy(low.at[1 - core], core, j).start()

    scale = jnp.exp(jnp.full((1, chunk), scale_ref[0], jnp.float32))
    offset = bias_ref[0]
    third = scale / (STEPS + 1)

    def weigh(side, other, j, own):
        logits = scale * lax.dot_general(
            low[side], other, (((1,), (1,)), ((), ())), preferred_element_type=jnp.float32
        ) + offset
        if own:
            same = lax.broadcasted_iota(jnp.int32, logits.shape, 0) == j * chunk + (
                lax.broadcasted_iota(jnp.int32, logits.shape, 1)
            )
            part = jax.nn.sigmoid(jnp.where(same, -logits, logits))
            coef = (jnp.where(same, -part, part) * third).astype(jnp.bfloat16)
        else:
            coef = (jax.nn.sigmoid(logits) * third).astype(jnp.bfloat16)
        return jnp.dot(coef, other, preferred_element_type=jnp.float32)

    def add_own(side):
        @pl.loop(0, PIECES // GROUP)
        def _(j):
            part = weigh(side, low[1 - side, pl.ds(j * chunk, chunk), :], j, True)

            @pl.when(j == 0)
            def _():
                total[side] = part

            @pl.when(j > 0)
            def _():
                total[side] += part

    def add_near(side, j):
        for i in range(GROUP):
            near_copy(low.at[0], side, j * GROUP + i).wait_recv()
        total[side] += weigh(side, near[side, pl.ds(j * chunk, chunk), :], j, False)

    def add_far(side, j):
        @pl.loop(j * GROUP, (j + 1) * GROUP)
        def _(i):
            far_copy(side, i, after).wait_recv()

            @pl.when(core == 1 - side)
            def _():
                near_copy(far.at[side], side, i).start()

        total[side] += weigh(side, far[side, pl.ds(j * chunk, chunk), :], j, False)

    def pass_on(first, last):
        @pl.when(middle)
        def _():
            @pl.loop(first, last)
            def _(j):
                @pl.when(relayed(j))
                def _():
                    relay_copy(j).wait_recv()

                    @pl.when(jnp.logical_not(bent))
                    def _():
                        onward_copy(j).start()

                    @pl.when(bent)
                    def _():
                        bent_copy(relay, pass_send.at[j], j).start()

    half = PIECES // 2
    pass_on(0, 1)
    add_own(0)

    @pl.when(waits)
    def _():
        pl.semaphore_wait(go_sem, 1)
        pl.loop(0, PIECES)(send_across)

        @pl.loop(AHEAD, PIECES)
        def _(j):
            send_along(1 - passing, j)

    pass_on(1, half)
    add_own(1)
    pass_on(half, half + 1)

    @pl.loop(0, PIECES // GROUP)
    def _(j):
        add_near(1 - core, j)

    pass_on(half + 1, PIECES)

    @pl.loop(0, PIECES)
    def _(j):
        @pl.when(bent_here(j))
        def _():
            bent_copy(low.at[0], bend_send.at[j], j).wait_recv()
            last_copy(j).start()

    lead = jnp.where(x == 0, 1, 0)

    @pl.loop(0, PIECES // GROUP)
    def _(j):
        add_far(lead, j)
        add_far(1 - lead, j)
        add_near(core, j)

    for side, out in enumerate((image_out, text_out)):

        @pl.loop(0, PIECES)
        def _(j):
            span = pl.ds(j * size, size)
            inv = inverse[side, span, :]
            unit = raw[side, span, :].astype(jnp.float32) * inv
            grad = total[side, span, :]
            along = jnp.sum(unit * grad, axis=-1, keepdims=True)
            out[span, :] = ((grad - unit * along) * inv).astype(jnp.bfloat16)

    @pl.loop(0, PIECES)
    def _(j):
        for side in range(2):
            far_copy(side, j, after).wait_send()
            near_copy(low.at[0], side, j).wait_send()

        @pl.when(jnp.logical_and(middle, relayed(j)))
        def _():
            onward_copy(j).wait_send()

        @pl.when(bent_here(j))
        def _():
            last_copy(j).wait_send()


def on_device(images, texts, log_scale, bias):
    rows, width = images.shape
    n = lax.axis_size("gx") * lax.axis_size("gy")
    block = (2, rows, width)
    dma = pltpu.SemaphoreType.DMA
    return pl.pallas_call(
        functools.partial(kernel, n),
        out_shape=[jax.ShapeDtypeStruct((rows, width), jnp.bfloat16)] * 2,
        in_specs=[pl.BlockSpec(memory_space=pltpu.SMEM)] * 2 + [pl.BlockSpec(memory_space=pltpu.HBM)] * 2,
        out_specs=[pl.BlockSpec(memory_space=pltpu.VMEM)] * 2,
        scratch_shapes=[
            pltpu.VMEM(block, jnp.bfloat16),
            pltpu.VMEM(block, jnp.bfloat16),
            pltpu.VMEM((2, rows, 1), jnp.float32),
            pltpu.VMEM(block, jnp.float32),
            pltpu.VMEM(block, jnp.bfloat16),
            pltpu.VMEM(block, jnp.bfloat16),
            pltpu.VMEM((rows, width), jnp.bfloat16),
            pltpu.VMEM((rows, width), jnp.bfloat16),
            dma((2, PIECES // GROUP)),
            dma((2, PIECES)),
            dma((2, PIECES)),
            dma((2, PIECES)),
            dma((2, PIECES)),
            dma((PIECES,)),
            dma((PIECES,)),
            dma((PIECES,)),
            dma((PIECES,)),
            pltpu.SemaphoreType.REGULAR,
        ],
        compiler_params=pltpu.CompilerParams(
            collective_id=0, has_side_effects=True, vmem_limit_bytes=51 * 1024 * 1024
        ),
        cost_estimate=pl.CostEstimate(
            flops=24 * rows * rows * width, bytes_accessed=8 * rows * width, transcendentals=6 * rows * rows
        ),
        name="contrast",
    )(log_scale, bias, images, texts)


def solution(mesh):
    return jax.shard_map(
        on_device,
        mesh=mesh,
        in_specs=(P(("gx", "gy"), None), P(("gx", "gy"), None), P(), P()),
        out_specs=(P(("gx", "gy"), None), P(("gx", "gy"), None)),
        check_vma=False,
    )
```

```python
import functools

import jax
import jax.numpy as jnp
from jax import lax
from jax.experimental import pallas as pl
from jax.experimental.pallas import tpu as pltpu
from jax.sharding import PartitionSpec as P

STEPS = 2
MESH = pl.DeviceIdType.MESH
PIECES = 8
GROUP = 4
CHUNKS = PIECES // GROUP


def kernel(
    n, scale_ref, bias_ref, images_ref, texts_ref, image_out, text_out,
    raw, low, inverse, total, far, near, relay, bend,
    load_sem, far_send, far_recv, near_send, near_recv, pass_send, pass_recv,
    bend_send, bend_recv, go_sem,
):
    rows, width = raw.shape[1:]
    size = rows // PIECES
    chunk = size * GROUP
    gx, gy = lax.axis_index("gx"), lax.axis_index("gy")
    inner = lax.axis_size("gy")
    me = gx * inner + gy
    core = lax.rem(gy, 2)
    x = lax.rem(gy // 2, 4)
    edge = jnp.logical_or(x == 0, x == 3)
    middle = jnp.logical_not(edge)
    early = gy < inner // 2
    waits = jnp.logical_and(edge, early)
    opens = jnp.logical_and(edge, jnp.logical_not(early))

    def at(distance):
        there = lax.rem(me + distance + n, n)
        return (there // inner, lax.rem(there, inner))

    sibling = (gx, gy + 1 - 2 * core)
    after, before = at(2), at(-2)
    across = at(jnp.where(x == 3, 2, -2))
    helper = at(jnp.where(x == 3, -4, 4))
    helped = at(jnp.where(x == 1, 4, -4))
    onward = at(jnp.where(x == 1, 6, -6))
    passing = 1 - lax.rem(x, 2)

    y, z = lax.rem(gx, 8), gx // 8 + 4 * (gy // 8)
    forth, back = passing == 0, passing == 1
    bent = jnp.logical_or(
        jnp.logical_and(forth, jnp.logical_and(y == 7, z == 5)),
        jnp.logical_and(back, jnp.logical_and(y == 0, z == 2)),
    )
    bends = jnp.logical_and(z == 0, y == 7 * passing)
    corner = (7 * passing, lax.rem(gy, 8))
    bent_from = (jnp.where(forth, 15, 16), jnp.where(forth, lax.rem(gy, 8) + 8, lax.rem(gy, 8)))
    bent_to = (jnp.where(forth, 16, 15), jnp.where(forth, core, 14 + core))

    barrier = pltpu.get_barrier_semaphore()
    pl.semaphore_signal(barrier, inc=1, device_id=sibling, device_id_type=MESH)
    for partner, last in ((after, 3), (before, 0)):

        @pl.when(jnp.logical_not(jnp.logical_and(opens, x == last)))
        def _():
            pl.semaphore_signal(barrier, inc=1, device_id=partner, device_id_type=MESH)

    @pl.when(middle)
    def _():
        pl.semaphore_signal(barrier, inc=1, device_id=helped, device_id_type=MESH)

    @pl.when(bends)
    def _():
        pl.semaphore_signal(barrier, inc=1, device_id=bent_from, device_id_type=MESH)

    greetings = 3 + edge.astype(jnp.int32) - waits.astype(jnp.int32) + bent.astype(jnp.int32)

    def load(ref, index, g):
        span = pl.ds(g * chunk, chunk)
        return pltpu.make_async_copy(ref.at[span], raw.at[index, span], load_sem.at[index, g])

    first = jnp.where(opens, 1 - passing, passing)
    for turn in range(2):
        for index, ref in enumerate((images_ref, texts_ref)):

            @pl.when(index == (first if turn == 0 else 1 - first))
            def _():
                for g in range(rows // chunk):
                    load(ref, index, g).start()

    def wait_load(index, j):
        @pl.when(lax.rem(j, GROUP) == 0)
        def _():
            load(images_ref, index, j // GROUP).wait()

    def rows_of(j, count=1):
        return pl.ds(j * size, count * size)

    def remote(source, target, send_sem, recv_sem, partner):
        return pltpu.make_async_remote_copy(
            src_ref=source,
            dst_ref=target,
            send_sem=send_sem,
            recv_sem=recv_sem,
            device_id=partner,
            device_id_type=MESH,
        )

    def far_copy(side, j, count, partner):
        span, c = rows_of(j, count), j // GROUP
        return remote(low.at[1 - side, span], far.at[side, span], far_send.at[side, c], far_recv.at[side, c], partner)

    def near_copy(source, side, c):
        span = rows_of(c * GROUP, GROUP)
        return remote(source.at[span], near.at[side, span], near_send.at[side, c], near_recv.at[side, c], sibling)

    def relay_copy(j):
        span = rows_of(j)
        return remote(low.at[1 - passing, span], relay.at[span], far_send.at[passing, j // GROUP], pass_recv.at[j], helper)

    def onward_copy(j, count=1):
        span = rows_of(j, count)
        return remote(relay.at[span], far.at[passing, span], pass_send, far_recv.at[passing, j // GROUP], onward)

    def bent_copy(source, send_sem, j):
        span = rows_of(j)
        return remote(source.at[span], bend.at[span], send_sem, bend_recv.at[j], corner)

    def last_copy(j, count=1):
        span = rows_of(j, count)
        return remote(bend.at[span], far.at[passing, span], bend_send, far_recv.at[passing, j // GROUP], bent_to)

    def relayed(j):
        return lax.rem(j, GROUP) < GROUP // 2

    def send_across(j):
        straight = jnp.logical_not(relayed(j))

        @pl.when(relayed(j))
        def _():
            relay_copy(j).start()

        @pl.when(jnp.logical_and(straight, jnp.logical_not(bent)))
        def _():
            far_copy(passing, j, 1, across).start()

        @pl.when(jnp.logical_and(straight, bent))
        def _():
            bent_copy(low.at[1 - passing], far_send.at[passing, j // GROUP], j).start()

    def normalize(index, j):
        span = pl.ds(j * size, size)
        values = raw[index, span, :].astype(jnp.float32)
        inv = lax.rsqrt(jnp.sum(values * values, axis=-1, keepdims=True) + 1e-06)
        inverse[index, span, :] = inv
        low[index, span, :] = (values * inv).astype(jnp.bfloat16)

    def send_along(side, j, count):
        for fixed, partner in enumerate((after, before)):

            @pl.when(side == fixed)
            def _():
                far_copy(fixed, j, count, partner).start()

    def enter(j):
        @pl.when(j == 0)
        def _():
            pl.semaphore_wait(barrier, greetings)

            @pl.when(opens)
            def _():
                pl.semaphore_signal(go_sem, inc=1, device_id=across, device_id_type=MESH)

    @pl.loop(0, PIECES)
    def _(j):
        wait_load(first, j)
        normalize(first, j)
        enter(j)

        @pl.when(opens)
        def _():
            send_across(j)

        @pl.when(jnp.logical_and(lax.rem(j, 2) == 1, jnp.logical_or(middle, jnp.logical_and(waits, j < GROUP))))
        def _():
            send_along(1 - first, j - 1, 2)

    @pl.loop(0, PIECES)
    def _(j):
        wait_load(1 - first, j)
        normalize(1 - first, j)

        @pl.when(jnp.logical_and(lax.rem(j, 2) == 1, jnp.logical_or(middle, opens)))
        def _():
            send_along(first, j - 1, 2)

    for c in range(CHUNKS):
        near_copy(low.at[1 - core], core, c).start()

    scale = jnp.exp(jnp.full((1, chunk), scale_ref[0], jnp.float32))
    offset = bias_ref[0]
    third = scale / (STEPS + 1)

    def weigh(side, other, j, own):
        logits = scale * lax.dot_general(
            low[side], other, (((1,), (1,)), ((), ())), preferred_element_type=jnp.float32
        ) + offset
        if own:
            same = lax.broadcasted_iota(jnp.int32, logits.shape, 0) == j * chunk + (
                lax.broadcasted_iota(jnp.int32, logits.shape, 1)
            )
            part = jax.nn.sigmoid(jnp.where(same, -logits, logits))
            coef = (jnp.where(same, -part, part) * third).astype(jnp.bfloat16)
        else:
            coef = (jax.nn.sigmoid(logits) * third).astype(jnp.bfloat16)
        return jnp.dot(coef, other, preferred_element_type=jnp.float32)

    def add_own(side):
        @pl.loop(0, CHUNKS)
        def _(j):
            part = weigh(side, low[1 - side, pl.ds(j * chunk, chunk), :], j, True)

            @pl.when(j == 0)
            def _():
                total[side] = part

            @pl.when(j > 0)
            def _():
                total[side] += part

    def add_near(side, c):
        near_copy(low.at[0], side, c).wait_recv()
        total[side] += weigh(side, near[side, rows_of(c * GROUP, GROUP), :], c, False)

    def add_far(c):
        j = c * GROUP
        far_copy(1 - core, j, GROUP, after).wait_recv()
        near_copy(far.at[1 - core], 1 - core, c).start()
        far_copy(core, j, GROUP, after).wait_recv()
        for side in range(2):
            total[side] += weigh(side, far[side, rows_of(j, GROUP), :], c, False)
        add_near(core, c)

    def pass_on(i):
        @pl.when(middle)
        def _():
            j = i // 2 * GROUP + i % 2
            relay_copy(j).wait_recv()

            @pl.when(jnp.logical_not(bent))
            def _():
                onward_copy(j).start()

            @pl.when(bent)
            def _():
                bent_copy(relay, pass_send, j).start()

    pass_on(0)
    add_own(0)

    @pl.when(waits)
    def _():
        pl.semaphore_wait(go_sem, 1)
        pl.loop(0, PIECES)(send_across)
        send_along(1 - passing, GROUP, GROUP)

    pass_on(1)
    add_own(1)
    pass_on(2)

    @pl.loop(0, CHUNKS)
    def _(c):
        add_near(1 - core, c)

    pass_on(3)

    @pl.loop(0, CHUNKS)
    def _(c):
        add_far(c)

        @pl.when(jnp.logical_and(bends, c == 0))
        def _():
            @pl.loop(0, PIECES)
            def _(j):
                @pl.when(relayed(j) == middle)
                def _():
                    bent_copy(relay, bend_send, j).wait_recv()
                    last_copy(j).start()

    for side, out in enumerate((image_out, text_out)):

        @pl.loop(0, PIECES)
        def _(j):
            span = pl.ds(j * size, size)
            inv = inverse[side, span, :]
            unit = raw[side, span, :].astype(jnp.float32) * inv
            grad = total[side, span, :]
            along = jnp.sum(unit * grad, axis=-1, keepdims=True)
            out[span, :] = ((grad - unit * along) * inv).astype(jnp.bfloat16)

    for side in range(2):
        for c in range(CHUNKS):
            far_copy(side, c * GROUP, GROUP, after).wait_send()
            near_copy(low.at[0], side, c).wait_send()

    @pl.when(middle)
    def _():
        onward_copy(0, GROUP).wait_send()

    @pl.when(bends)
    def _():
        last_copy(0, GROUP).wait_send()


def on_device(images, texts, log_scale, bias):
    rows, width = images.shape
    n = lax.axis_size("gx") * lax.axis_size("gy")
    block = (2, rows, width)
    dma = pltpu.SemaphoreType.DMA
    return pl.pallas_call(
        functools.partial(kernel, n),
        out_shape=[jax.ShapeDtypeStruct((rows, width), jnp.bfloat16)] * 2,
        in_specs=[pl.BlockSpec(memory_space=pltpu.SMEM)] * 2 + [pl.BlockSpec(memory_space=pltpu.HBM)] * 2,
        out_specs=[pl.BlockSpec(memory_space=pltpu.VMEM)] * 2,
        scratch_shapes=[
            pltpu.VMEM(block, jnp.bfloat16),
            pltpu.VMEM(block, jnp.bfloat16),
            pltpu.VMEM((2, rows, 1), jnp.float32),
            pltpu.VMEM(block, jnp.float32),
            pltpu.VMEM(block, jnp.bfloat16),
            pltpu.VMEM(block, jnp.bfloat16),
            pltpu.VMEM((rows, width), jnp.bfloat16),
            pltpu.VMEM((rows, width), jnp.bfloat16),
            dma((2, CHUNKS)),
            dma((2, CHUNKS)),
            dma((2, CHUNKS)),
            dma((2, CHUNKS)),
            dma((2, CHUNKS)),
            dma,
            dma((PIECES,)),
            dma,
            dma((PIECES,)),
            pltpu.SemaphoreType.REGULAR,
        ],
        compiler_params=pltpu.CompilerParams(
            collective_id=0, has_side_effects=True, vmem_limit_bytes=51 * 1024 * 1024
        ),
        cost_estimate=pl.CostEstimate(
            flops=24 * rows * rows * width, bytes_accessed=8 * rows * width, transcendentals=6 * rows * rows
        ),
        name="contrast",
    )(log_scale, bias, images, texts)


def solution(mesh):
    return jax.shard_map(
        on_device,
        mesh=mesh,
        in_specs=(P(("gx", "gy"), None), P(("gx", "gy"), None), P(), P()),
        out_specs=(P(("gx", "gy"), None), P(("gx", "gy"), None)),
        check_vma=False,
    )
```
